128 devices in a mesh: grp: 2 (over core), dp: 4 (over z), ep: 16 (over x, y).
Axes of the slice: x: 4, y: 4, z: 4, core: 2. Of those that a mesh axis runs over, the one named last changes fastest.
Arguments:
- tokens: bfloat16 [2048, 2048], P(('grp', 'dp', 'ep')), may hold values from -6 to 6
- think_gain: float32 [2048], replicated, may hold values from 0.1 to 1.9
- think_routes: int32 [2048, 8], P(('grp', 'dp', 'ep')), may hold values from 0 to 127, all different within a row; in each aligned block of 16 rows (0 to 15, 16 to 31, ...) at most 2 rows name the same one
- think_weights: float32 [2048, 8], P(('grp', 'dp', 'ep')), may hold values from 0.1 to 1
- think_keep: int32 [2048, 8], P(('grp', 'dp', 'ep')), may hold values 0 or 1
- think_gate_up: bfloat16 [128, 2048, 1536], P(('grp', 'dp', 'ep')), may hold values from -0.125 to 0.125
- think_down: bfloat16 [128, 768, 2048], P(('grp', 'dp', 'ep')), may hold values from -0.21875 to 0.21875
- talk_proj: bfloat16 [2048, 1024], replicated, may hold values from -0.125 to 0.125
- codec_table: bfloat16 [3072, 1024], replicated, may hold values from -6 to 6
- codec_ids: int32 [2048], P(('grp', 'dp', 'ep')), may hold values from 0 to 3071
- talk_gain: float32 [1024], replicated, may hold values from 0.1 to 1.9
- talk_routes: int32 [2048, 8], P(('grp', 'dp', 'ep')), may hold values from 0 to 127, all different within a row; in each aligned block of 16 rows (0 to 15, 16 to 31, ...) at most 2 rows name the same one
- talk_weights: float32 [2048, 8], P(('grp', 'dp', 'ep')), may hold values from 0.1 to 1
- talk_keep: int32 [2048, 8], P(('grp', 'dp', 'ep')), may hold values 0 or 1
- talk_gate_up: bfloat16 [128, 1024, 768], P(('grp', 'dp', 'ep')), may hold values from -0.1875 to 0.1875
- talk_down: bfloat16 [128, 384, 1024], P(('grp', 'dp', 'ep')), may hold values from -0.3125 to 0.3125
Outputs:
- think_out: bfloat16 [2048, 2048], P(('grp', 'dp', 'ep'))
- talk_out: bfloat16 [2048, 1024], P(('grp', 'dp', 'ep'))
The draws below stay inside these ranges and needn't reach their ends.
Inputs may be any that keep to these rules, and one draw needn't show every extreme that they name: `think_routes`: within the rows of one device, no expert is named more than 2 times, a bound that some block reaches. `talk_routes`: within the rows of one device, no expert is named more than 2 times, a bound that some block reaches.
All inputs are finite; a program needn't handle non-finite values. No bound on the sum of `think_keep` or of `talk_keep` on one device may be relied on, other than what follows from the above.
Results may differ from the reference program's by a relative error of at most 0.006.
Values may be sent and summed in bfloat16 or wider, within the bound.
A program may use at most 64 MiB of HBM per device.

```python
import math
import jax
import jax.numpy as jnp
import numpy as np
from jax import lax

D = 2048
FF = 768
TALK_D = 1024
TALK_FF = 384
CODEC_VOCAB = 3072
TOP = 8
TOK_DEV = 16
EXPERTS = 128
CAP = 2
TOKENS = 2048


def touch_ends(result, rng, low, top_value):
    extent = result.shape
    spot = [jax.random.randint(jax.random.fold_in(rng, axis), (), 0, extent[axis]) for axis in range(len(extent))]
    result = result.at[tuple(spot)].set(low)
    longest = extent.index(max(extent))
    spot[longest] = (spot[longest] + 1) % extent[longest]
    return result.at[tuple(spot)].set(top_value)


def steps_of(rng, dims, split, least, high):
    level, own = 1.0, jax.random.fold_in(rng, 6)
    for axis_at, shards_of in split:
        heights = jnp.exp(jax.random.uniform(jax.random.fold_in(own, axis_at), (shards_of,), jnp.float32, least / len(split), high / len(split)))
        level = level * jnp.repeat(heights, dims[axis_at] // shards_of).reshape([-1 if axis == axis_at else 1 for axis in range(len(dims))])
    return level


def assign_block(stream_key, own, number, rows, count, top, reach, slope):
    ranking = jax.random.permutation(stream_key, count)
    heavy_load, common = load_shares(count, rows * top, reach, slope, True), load_shares(count, rows * top, reach, slope, False)
    places = jnp.arange(count)

    def named(tallies, rotation):
        used = int((tallies > 0).sum())
        fixed = max(1, used // 4)
        passed = fixed + (places - fixed + rotation * (used - fixed)) % max(1, count - fixed)
        return jnp.zeros((count,), jnp.int32).at[ranking[jnp.where(places < fixed, places, passed)]].set(jnp.asarray(tallies, jnp.int32))

    tallies = jnp.where(number % 4 == 0, named(heavy_load, number // 4), named(common, number - number // 4 - 1))
    mixed = jax.random.permutation(jax.random.fold_in(own, 3), count)
    source_of, taker = mixed[0:count // 2 * 2:2], mixed[1:count // 2 * 2:2]
    margin = jnp.minimum(tallies[source_of] - 1, reach - tallies[taker]) // 2
    margin = jnp.where((source_of == ranking[0]) | (taker == ranking[0]) | (tallies[taker] == 0), 0, jnp.maximum(margin, 0))
    passed = jax.random.randint(jax.random.fold_in(own, 4), (count // 2,), 0, 1 << 20) % (margin + 1)
    tallies = tallies.at[source_of].add(-passed).at[taker].add(passed)
    items = jnp.searchsorted(jnp.cumsum(tallies), jnp.arange(rows * top), side="right").astype(jnp.int32)
    grid = items.reshape(top, rows).T
    grid = grid[jax.random.permutation(jax.random.fold_in(own, 1), rows)]
    rotation = jax.random.randint(jax.random.fold_in(own, 2), (rows, 1), 0, top)
    return jnp.take_along_axis(grid, (jnp.arange(top)[None, :] + rotation) % top, axis=1)


def load_shares(count, total, limit, skew, full):
    portions = [(1 << 20) // math.isqrt(standing ** skew) + 1 for standing in range(1, count + 1)]
    largest = limit if full else min(limit, max(-(-total // count), total * portions[0] // sum(portions)))
    least = 1 if total - largest >= count - 1 else 0
    given, rest = [largest] + [least] * (count - 1), total - largest - least * (count - 1)
    while rest > 0:
        candidates = [i for i in range(1, count) if given[i] < largest] or [i for i in range(1, count) if given[i] < limit]
        pool, remaining = sum([portions[i] for i in candidates]), rest
        for i in candidates:
            extra = min(limit - given[i], max(1, remaining * portions[i] // pool), rest)
            given[i] = given[i] + extra
            rest = rest - extra
    return np.array(given)


def normal_values(stream_key, dims, scale, most, cuts=(), held_as=jnp.bfloat16):
    level = steps_of(stream_key, dims, cuts, -0.22, 0.18) if cuts else 1.0
    drawn = jax.random.normal(stream_key, dims, jnp.float32) * scale * level
    return jnp.minimum(jnp.maximum(drawn, -most), most).astype(held_as)


def setup_inputs(seed: int = 0) -> dict:
    seeds = jax.random.split(jax.random.key(seed), 17)
    tokens = normal_values(seeds[0], (TOKENS, D), 1.0, 6.0, ((0, 128),))
    think_gain = jnp.clip(1.0 + 0.18 * jax.random.normal(seeds[1], (D,), jnp.float32), 0.1, 1.9)
    think_routes_keys = jax.random.split(jax.random.fold_in(seeds[2], 1), TOKENS // TOK_DEV)
    think_routes_turns = jax.random.permutation(jax.random.fold_in(seeds[2], 3), TOKENS // TOK_DEV)
    think_routes = jax.vmap(lambda own, number: assign_block(jax.random.fold_in(seeds[2], 2), own, number, TOK_DEV, EXPERTS, TOP, CAP, 2))(think_routes_keys, think_routes_turns).reshape((TOKENS, TOP))
    think_weights = jnp.clip(jnp.exp(math.log(1.0) - 2.3025851 * jax.random.uniform(seeds[3], (TOKENS, TOP), jnp.float32) ** steps_of(seeds[3], (TOKENS, TOP), ((0, 128),), -0.2, 0.2)), 0.1, 1.0)
    think_keep = touch_ends((jax.random.randint(seeds[4], (TOKENS, TOP), 0, 8) < 7).astype(jnp.int32), jax.random.fold_in(seeds[4], 1), 0, 1)
    think_gate_up = normal_values(seeds[5], (EXPERTS, D, 2 * FF), D ** -0.5, 0.125, ((0, 128),))
    think_down = normal_values(seeds[6], (EXPERTS, FF, D), FF ** -0.5, 0.21875, ((0, 128),))
    talk_proj = normal_values(seeds[7], (D, TALK_D), D ** -0.5, 0.125)
    codec_table = normal_values(seeds[8], (CODEC_VOCAB, TALK_D), 1.0, 6.0)
    codec_ids = touch_ends(jax.random.randint(seeds[9], (TOKENS,), 0, CODEC_VOCAB), jax.random.fold_in(seeds[9], 1), 0, CODEC_VOCAB - 1).astype(jnp.int32)
    talk_gain = jnp.clip(1.0 + 0.18 * jax.random.normal(seeds[10], (TALK_D,), jnp.float32), 0.1, 1.9)
    talk_routes_keys = jax.random.split(jax.random.fold_in(seeds[11], 1), TOKENS // TOK_DEV)
    talk_routes_turns = jax.random.permutation(jax.random.fold_in(seeds[11], 3), TOKENS // TOK_DEV)
    talk_routes = jax.vmap(lambda own, number: assign_block(jax.random.fold_in(seeds[11], 2), own, number, TOK_DEV, EXPERTS, TOP, CAP, 2))(talk_routes_keys, talk_routes_turns).reshape((TOKENS, TOP))
    talk_weights = jnp.clip(jnp.exp(math.log(1.0) - 2.3025851 * jax.random.uniform(seeds[12], (TOKENS, TOP), jnp.float32) ** steps_of(seeds[12], (TOKENS, TOP), ((0, 128),), -0.2, 0.2)), 0.1, 1.0)
    talk_keep = touch_ends((jax.random.randint(seeds[13], (TOKENS, TOP), 0, 8) < 7).astype(jnp.int32), jax.random.fold_in(seeds[13], 1), 0, 1)
    talk_gate_up = normal_values(seeds[14], (EXPERTS, TALK_D, 2 * TALK_FF), TALK_D ** -0.5, 0.1875, ((0, 128),))
    talk_down = normal_values(seeds[15], (EXPERTS, TALK_FF, TALK_D), TALK_FF ** -0.5, 0.3125, ((0, 128),))
    return {"tokens": tokens, "think_gain": think_gain, "think_routes": think_routes, "think_weights": think_weights, "think_keep": think_keep, "think_gate_up": think_gate_up, "think_down": think_down, "talk_proj": talk_proj, "codec_table": codec_table, "codec_ids": codec_ids, "talk_gain": talk_gain, "talk_routes": talk_routes, "talk_weights": talk_weights, "talk_keep": talk_keep, "talk_gate_up": talk_gate_up, "talk_down": talk_down}


def normed(inputs, norm_gain):
    values = inputs.astype(jnp.float32)
    inverse_rms = lax.rsqrt(lax.optimization_barrier(jnp.mean(values * values, axis=-1, keepdims=True)) + 1e-06)
    return (values * inverse_rms * norm_gain.astype(jnp.float32)).astype(jnp.bfloat16)

def positions_of(routes):
    block_count = routes.shape[0] // TOK_DEV
    flat_routes = routes.reshape(block_count, TOK_DEV * TOP).astype(jnp.int32)
    matches = (flat_routes[:, :, None] == jnp.arange(EXPERTS, dtype=jnp.int32)[None, None, :]).astype(jnp.int32)
    earlier = (jnp.cumsum(matches, axis=1) - matches).astype(jnp.int32)
    slot_index = lax.optimization_barrier(jnp.sum(earlier * matches, axis=2)).astype(jnp.int32)
    block_index = jnp.arange(block_count, dtype=jnp.int32)[:, None]
    destination = flat_routes * (block_count * CAP) + block_index * CAP + slot_index
    return destination.reshape(-1).astype(jnp.int32)

def expert_layer(normed_rows, routes, gate_up, down_proj):
    row_width = normed_rows.shape[1]
    block_count = normed_rows.shape[0] // TOK_DEV
    destination = positions_of(routes)
    repeated = jnp.repeat(normed_rows, TOP, axis=0)
    bin_rows = jnp.zeros((EXPERTS * block_count * CAP, row_width), jnp.bfloat16).at[destination].set(repeated)
    bin_rows = bin_rows.reshape(EXPERTS, block_count * CAP, row_width)

    def per_expert(operands):
        received, weight_up, weight_down = operands
        joined = jnp.dot(received, weight_up, preferred_element_type=jnp.float32)
        split_at = weight_up.shape[1] // 2
        hidden_act = (jax.nn.silu(joined[:, :split_at]) * joined[:, split_at:]).astype(jnp.bfloat16)
        return jnp.dot(hidden_act, weight_down, preferred_element_type=jnp.float32).astype(jnp.bfloat16)
    results = lax.map(per_expert, (bin_rows, gate_up, down_proj))
    return results.reshape(-1, row_width)[destination].reshape(normed_rows.shape[0], TOP, row_width)

def mix_back(residual, returned, weights, keep):
    shares = weights.astype(jnp.float32) * keep.astype(jnp.float32) / lax.optimization_barrier(jnp.sum(weights.astype(jnp.float32), axis=1, keepdims=True))
    return residual.astype(jnp.float32) + lax.optimization_barrier(jnp.sum(shares[:, :, None] * returned.astype(jnp.float32), axis=1))

def reference(tokens, think_gain, think_routes, think_weights, think_keep, think_gate_up, think_down, talk_proj, codec_table, codec_ids, talk_gain, talk_routes, talk_weights, talk_keep, talk_gate_up, talk_down):
    think_norm = normed(tokens, think_gain)
    think_expert = expert_layer(think_norm, think_routes, think_gate_up, think_down)
    think_out = mix_back(tokens, think_expert, think_weights, think_keep).astype(jnp.bfloat16)
    talk_input = jnp.dot(think_out, talk_proj, preferred_element_type=jnp.float32) + codec_table[codec_ids].astype(jnp.float32)
    talk_norm = normed(talk_input, talk_gain)
    talk_expert = expert_layer(talk_norm, talk_routes, talk_gate_up, talk_down)
    talk_out = mix_back(talk_input, talk_expert, talk_weights, talk_keep).astype(jnp.bfloat16)
    return (think_out, talk_out)
```

```python
import functools

import jax
import jax.numpy as jnp
import numpy as np
from jax import lax
from jax.experimental import pallas as pl
from jax.experimental.pallas import tpu as pltpu
from jax.sharding import PartitionSpec as P

MESH = pl.DeviceIdType.MESH
AXES = ("grp", "dp", "ep")
ROWS = 16
SLOT = 16
PARTNERS = 128
F32 = jnp.float32
BF16 = jnp.bfloat16


def partner_order():
    rng = np.random.default_rng(1)
    every = [(a, c, p, q) for a in range(2) for c in range(4) for p in range(4) for q in range(4)]
    shuffled = [every[i] for i in rng.permutation(len(every))]

    def hops(step):
        return sum(min(v, 4 - v) for v in step[1:]) + (0 if any(step) else -1)

    return sorted(shuffled, key=lambda step: -hops(step))


ORDER = partner_order()
CHUNKS = ((0, 128),)


def my_place():
    ep = lax.axis_index("ep")
    return lax.axis_index("grp"), lax.axis_index("dp"), ep // 4, ep % 4


def device_at(place, step, sign):
    grp, dp, x, y = place
    a, c, p, q = step
    if sign < 0:
        a, c, p, q = (-a) % 2, (-c) % 4, (-p) % 4, (-q) % 4
    return ((grp + a) % 2, (dp + c) % 4, ((x + p) % 4) * 4 + (y + q) % 4)


def iota(shape, dim):
    return lax.broadcasted_iota(jnp.int32, shape, dim)


def dot(a, b):
    return jnp.dot(a, b, preferred_element_type=F32)


def rms_rows(values, gain):
    inverse = lax.rsqrt(jnp.mean(values * values, axis=-1, keepdims=True) + 1e-06)
    return (values * inverse * gain).astype(BF16)


def route_tables(place, steps, routes, weights, keep, pick_ref, mix_ref):
    grp, dp, x, y = place
    expert = (
        (((grp + steps // 64) & 1) * 4 + ((dp + (steps // 16) % 4) & 3)) * 16
        + ((x + (steps // 4) % 4) & 3) * 4
        + ((y + steps % 4) & 3)
    )
    shares = weights * keep.astype(F32) / jnp.sum(weights, axis=1, keepdims=True)
    named = jnp.zeros((ROWS, PARTNERS), F32)
    share = jnp.zeros((ROWS, PARTNERS), F32)
    for k in range(routes.shape[1]):
        match = routes[:, k : k + 1] == expert
        named = named + jnp.where(match, 1.0, 0.0)
        share = share + jnp.where(match, shares[:, k : k + 1], 0.0)
    below = (iota((ROWS, ROWS), 1) < iota((ROWS, ROWS), 0)).astype(F32).astype(BF16)
    code = named * (1.0 + dot(below, named.astype(BF16)))
    high = share.astype(BF16)
    low = (share - high.astype(F32)).astype(BF16)
    wide = PARTNERS * SLOT
    spread = jnp.where(iota((PARTNERS, wide), 1) // SLOT == iota((PARTNERS, wide), 0), 1.0, 0.0).astype(BF16)
    stacked = jnp.concatenate([code.astype(BF16), high, low], axis=0)
    lanes = dot(stacked, spread)
    lane = iota((ROWS, wide), 1)
    chosen = lanes[:ROWS] == ((lane & 1) + 1).astype(F32)
    parts = (
        jnp.where(chosen, 1.0, 0.0),
        jnp.where(chosen, lanes[ROWS : 2 * ROWS], 0.0),
        jnp.where(chosen, lanes[2 * ROWS :], 0.0),
    )
    block = (lane >> 1) & 7
    for c in range(8):
        here = block == c
        pick_ref[c * ROWS : (c + 1) * ROWS, :] = jnp.where(here, parts[0], 0.0).astype(BF16)
        mix_ref[c * ROWS : (c + 1) * ROWS, :] = jnp.where(here, parts[1], 0.0).astype(BF16)
        mix_ref[128 + c * ROWS : 128 + (c + 1) * ROWS, :] = jnp.where(here, parts[2], 0.0).astype(BF16)


def by_blocks(rows, halves):
    return jnp.concatenate(
        [
            jnp.concatenate(
                [rows[:, h * 1024 + c * 128 : h * 1024 + (c + 1) * 128] for h in range(halves)], axis=1
            )
            for c in range(8)
        ],
        axis=0,
    )


def unblock(blocks, halves):
    return jnp.concatenate(
        [
            blocks[c * ROWS : (c + 1) * ROWS, h * 128 : (h + 1) * 128]
            for h in range(halves)
            for c in range(8)
        ],
        axis=1,
    )


def copy_to(source, target, device, send_sem, recv_sem):
    return pltpu.make_async_remote_copy(
        src_ref=source,
        dst_ref=target,
        send_sem=send_sem,
        recv_sem=recv_sem,
        device_id=device,
        device_id_type=MESH,
    )


def wait_bytes(ref, first, last, sem):
    part = ref.at[pl.ds(first * SLOT, (last - first) * SLOT)]
    pltpu.make_async_copy(part, part, sem).wait()


def expert_layer(place, normed, halves, pick, mix, gate_up, down, wait_weights, idle, bufs, sems):
    bins, arrived, rows, hidden, results, packed, returned = bufs
    there_send, there_recv, back_send, back_recv = sems
    width = halves * 1024
    blocks = by_blocks(normed, halves)
    for g in range(8):
        lanes = pl.ds(g * 256, 256)
        bins[lanes, :] = lax.dot_general(
            pick[:, lanes], blocks, (((0,), (0,)), ((), ())), preferred_element_type=F32
        ).astype(BF16)
        for j in range(g * 16, min(g * 16 + 16, PARTNERS - 1)):
            part = pl.ds(j * SLOT, SLOT)
            copy_to(
                bins.at[part], arrived.at[part], device_at(place, ORDER[j], 1), there_send, there_recv.at[chunk_of(j)]
            ).start()
    own = pl.ds((PARTNERS - 1) * SLOT, SLOT)
    arrived[own, :] = bins[own, :]

    out_row, in_row = iota((256, 256), 0), iota((256, 256), 1)
    unpack = jnp.where(((out_row // 2) % 16) * 16 + (out_row // 32) * 2 + out_row % 2 == in_row, 1.0, 0.0).astype(BF16)
    pack = jnp.where(((in_row // 2) % 16) * 16 + (in_row // 32) * 2 + in_row % 2 == out_row, 1.0, 0.0).astype(BF16)
    hidden_width = down.shape[1]
    idle()
    wait_weights()
    for k, (first, last) in enumerate(CHUNKS):
        wait_bytes(arrived, first, min(last, PARTNERS - 1), there_recv.at[k])
        for g in range(first // 16, last // 16):
            group = dot(unpack, arrived[g * 256 : (g + 1) * 256, :]).astype(BF16)
            for h in range(halves):
                for c in range(8):
                    rows[g * 32 : (g + 1) * 32, h * 1024 + c * 128 : h * 1024 + (c + 1) * 128] = group[
                        c * 32 : (c + 1) * 32, h * 128 : (h + 1) * 128
                    ]
        span = slice(first * 2, last * 2)
        tile = 256 if hidden_width % 256 == 0 else 128
        for n in range(hidden_width // tile):
            gate = dot(rows[span, :], gate_up[0, :, n * tile : (n + 1) * tile])
            up = dot(rows[span, :], gate_up[0, :, hidden_width + n * tile : hidden_width + (n + 1) * tile])
            hidden[span, n * tile : (n + 1) * tile] = (gate / (1.0 + jnp.exp(-gate)) * up).astype(BF16)
        for n in range(width // 256):
            results[span, n * 256 : (n + 1) * 256] = dot(
                hidden[span, :], down[0, :, n * 256 : (n + 1) * 256]
            ).astype(BF16)
        for g in range(first // 16, last // 16):
            stacked = jnp.concatenate(
                [
                    jnp.concatenate(
                        [
                            results[g * 32 : (g + 1) * 32, h * 1024 + c * 128 : h * 1024 + (c + 1) * 128]
                            for h in range(halves)
                        ],
                        axis=1,
                    )
                    for c in range(8)
                ],
                axis=0,
            )
            packed[g * 256 : (g + 1) * 256, :] = dot(pack, stacked).astype(BF16)
            for j in range(g * 16, min(g * 16 + 16, PARTNERS - 1)):
                part = pl.ds(j * SLOT, SLOT)
                copy_to(
                    packed.at[part], returned.at[part], device_at(place, ORDER[j], -1), back_send, back_recv
                ).start()
    returned[own, :] = packed[own, :]
    wait_bytes(returned, 0, PARTNERS - 1, back_recv)
    total = dot(mix[...], returned[...])
    wait_bytes(bins, 0, PARTNERS - 1, there_send)
    wait_bytes(packed, 0, PARTNERS - 1, back_send)
    return unblock(total[:128] + total[128:], halves)


def chunk_of(j):
    return next(k for k, (first, last) in enumerate(CHUNKS) if first <= j < last)


def step_kernel(
    steps,
    tokens,
    think_gain,
    think_routes,
    think_weights,
    think_keep,
    codec_ids,
    talk_gain,
    talk_routes,
    talk_weights,
    talk_keep,
    think_gate_up,
    think_down,
    talk_proj,
    codec_table,
    talk_gate_up,
    talk_down,
    think_out,
    talk_out,
    gu1,
    dn1,
    proj,
    table,
    gu2,
    dn2,
    codec,
    pick1,
    mix1,
    pick2,
    mix2,
    bins1,
    arrived1,
    rows1,
    hidden1,
    results1,
    packed1,
    returned1,
    bins2,
    arrived2,
    rows2,
    hidden2,
    results2,
    packed2,
    returned2,
    load_sem,
    send_sem,
    there_recv,
    back_recv,
):
    place = my_place()
    barrier = pltpu.get_barrier_semaphore()
    for step in ORDER[:-1]:
        pl.semaphore_signal(barrier, inc=1, device_id=device_at(place, step, 1), device_id_type=MESH)

    loads = [
        pltpu.make_async_copy(source, target, load_sem.at[i])
        for i, (source, target) in enumerate(
            (
                (think_gate_up, gu1),
                (think_down, dn1),
                (codec_table, table),
                (talk_proj, proj),
                (talk_gate_up, gu2),
                (talk_down, dn2),
            )
        )
    ]
    for load in loads:
        load.start()

    partner = steps[...]
    normed = rms_rows(tokens[...].astype(F32), think_gain[...])
    route_tables(place, partner, think_routes[...], think_weights[...], think_keep[...], pick1, mix1)
    route_tables(place, partner, talk_routes[...], talk_weights[...], talk_keep[...], pick2, mix2)
    pl.semaphore_wait(barrier, PARTNERS - 1)

    def find_codec():
        loads[2].wait()
        vocab = table.shape[0]
        row = iota((ROWS, vocab), 0)
        ids = jnp.zeros((ROWS, vocab), jnp.int32)
        for t in range(ROWS):
            ids = jnp.where(row == t, codec_ids[t], ids)
        chosen = jnp.where(iota((ROWS, vocab), 1) == ids, 1.0, 0.0).astype(BF16)
        codec[...] = dot(chosen, table[...])

    def think_weights_ready():
        loads[0].wait()
        loads[1].wait()

    mixed = expert_layer(
        place,
        normed,
        2,
        pick1,
        mix1,
        gu1,
        dn1,
        think_weights_ready,
        find_codec,
        (bins1, arrived1, rows1, hidden1, results1, packed1, returned1),
        (send_sem.at[0], there_recv.at[0], send_sem.at[1], back_recv.at[0]),
    )
    think = (tokens[...].astype(F32) + mixed).astype(BF16)
    think_out[...] = think

    loads[3].wait()
    talk_input = dot(think, proj[...]) + codec[...]
    talk_normed = rms_rows(talk_input, talk_gain[...])

    def talk_weights_ready():
        loads[4].wait()
        loads[5].wait()

    mixed = expert_layer(
        place,
        talk_normed,
        1,
        pick2,
        mix2,
        gu2,
        dn2,
        talk_weights_ready,
        lambda: None,
        (bins2, arrived2, rows2, hidden2, results2, packed2, returned2),
        (send_sem.at[2], there_recv.at[1], send_sem.at[3], back_recv.at[1]),
    )
    talk_out[...] = (talk_input + mixed).astype(BF16)


def shards(
    tokens,
    think_gain,
    think_routes,
    think_weights,
    think_keep,
    think_gate_up,
    think_down,
    talk_proj,
    codec_table,
    codec_ids,
    talk_gain,
    talk_routes,
    talk_weights,
    talk_keep,
    talk_gate_up,
    talk_down,
):
    steps = jnp.asarray([[((a * 4 + c) * 4 + p) * 4 + q for a, c, p, q in ORDER]], jnp.int32)
    wide = PARTNERS * SLOT
    vmem = pl.BlockSpec(memory_space=pltpu.VMEM)
    smem = pl.BlockSpec(memory_space=pltpu.SMEM)
    hbm = pl.BlockSpec(memory_space=pl.ANY)

    def exchange(halves, hidden_width):
        width = halves * 1024
        return [
            pltpu.VMEM((wide, halves * 128), BF16),
            pltpu.VMEM((wide, halves * 128), BF16),
            pltpu.VMEM((256, width), BF16),
            pltpu.VMEM((256, hidden_width), BF16),
            pltpu.VMEM((256, width), BF16),
            pltpu.VMEM((wide, halves * 128), BF16),
            pltpu.VMEM((wide, halves * 128), BF16),
        ]

    return pl.pallas_call(
        step_kernel,
        out_shape=(
            jax.ShapeDtypeStruct(tokens.shape, BF16),
            jax.ShapeDtypeStruct((ROWS, talk_proj.shape[1]), BF16),
        ),
        in_specs=[vmem] * 6 + [smem] + [vmem] * 4 + [hbm] * 6,
        out_specs=(vmem, vmem),
        scratch_shapes=[
            pltpu.VMEM(think_gate_up.shape, BF16),
            pltpu.VMEM(think_down.shape, BF16),
            pltpu.VMEM(talk_proj.shape, BF16),
            pltpu.VMEM(codec_table.shape, BF16),
            pltpu.VMEM(talk_gate_up.shape, BF16),
            pltpu.VMEM(talk_down.shape, BF16),
            pltpu.VMEM((ROWS, talk_proj.shape[1]), F32),
            pltpu.VMEM((128, wide), BF16),
            pltpu.VMEM((256, wide), BF16),
            pltpu.VMEM((128, wide), BF16),
            pltpu.VMEM((256, wide), BF16),
        ]
        + exchange(2, think_down.shape[1])
        + exchange(1, talk_down.shape[1])
        + [
            pltpu.SemaphoreType.DMA((6,)),
            pltpu.SemaphoreType.DMA((4,)),
            pltpu.SemaphoreType.DMA((2, len(CHUNKS))),
            pltpu.SemaphoreType.DMA((2,)),
        ],
        compiler_params=pltpu.CompilerParams(
            collective_id=0, has_side_effects=True, vmem_limit_bytes=56 * 2**20
        ),
        name="moe_step",
    )(
        steps,
        tokens,
        think_gain.reshape(1, -1),
        think_routes,
        think_weights,
        think_keep,
        codec_ids,
        talk_gain.reshape(1, -1),
        talk_routes,
        talk_weights,
        talk_keep,
        think_gate_up,
        think_down,
        talk_proj,
        codec_table,
        talk_gate_up,
        talk_down,
    )


def solution(mesh):
    rows = P(AXES, None)
    experts = P(AXES, None, None)
    return jax.shard_map(
        shards,
        mesh=mesh,
        in_specs=(rows, P(), rows, rows, rows, experts, experts, P(), P(), P(AXES), P(), rows, rows, rows, experts, experts),
        out_specs=(rows, rows),
        check_vma=False,
    )
```

```python
import functools

import jax
import jax.numpy as jnp
import numpy as np
from jax import lax
from jax.experimental import pallas as pl
from jax.experimental.pallas import tpu as pltpu
from jax.sharding import PartitionSpec as P

MESH = pl.DeviceIdType.MESH
AXES = ("grp", "dp", "ep")
ROWS = 16
SLOT = 16
PARTNERS = 128
F32 = jnp.float32
BF16 = jnp.bfloat16


def hops(step):
    return sum(min(v, 4 - v) for v in step[1:])


def partner_order(distances):
    rng = np.random.default_rng(1)
    every = [(a, c, p, q) for a in range(2) for c in range(4) for p in range(4) for q in range(4)]
    shuffled = [every[i] for i in rng.permutation(len(every))]
    return sorted(shuffled, key=lambda step: distances.index(hops(step)) if any(step) else len(distances))


THINK_ORDER = partner_order((3, 6, 5, 4, 2, 1, 0))
TALK_ORDER = partner_order((6, 5, 4, 3, 2, 1, 0))
EARLY = sum(hops(step) == 3 for step in THINK_ORDER)
THINK_CHUNKS = ((0, 48), (48, 128))
TALK_CHUNKS = ((0, 48), (48, 128))
NEAR = [step for step in THINK_ORDER[:-1] if hops(step) <= 3]
RELAYS = ((0, 1, 1, 1), (0, 3, 3, 3))


def my_place():
    ep = lax.axis_index("ep")
    return lax.axis_index("grp"), lax.axis_index("dp"), ep // 4, ep % 4


def device_at(place, step, sign):
    grp, dp, x, y = place
    a, c, p, q = step
    if sign < 0:
        a, c, p, q = (-a) % 2, (-c) % 4, (-p) % 4, (-q) % 4
    return ((grp + a) % 2, (dp + c) % 4, ((x + p) % 4) * 4 + (y + q) % 4)


def iota(shape, dim):
    return lax.broadcasted_iota(jnp.int32, shape, dim)


def dot(a, b):
    return jnp.dot(a, b, preferred_element_type=F32)


def rms_rows(values, gain):
    inverse = lax.rsqrt(jnp.mean(values * values, axis=-1, keepdims=True) + 1e-06)
    return (values * inverse * gain).astype(BF16)


def route_tables(place, steps, routes, weights, keep, pick_ref, mix_ref):
    grp, dp, x, y = place
    expert = (
        (((grp + steps // 64) & 1) * 4 + ((dp + (steps // 16) % 4) & 3)) * 16
        + ((x + (steps // 4) % 4) & 3) * 4
        + ((y + steps % 4) & 3)
    )
    shares = jnp.transpose(weights * keep.astype(F32) / jnp.sum(weights, axis=0, keepdims=True))
    routes = jnp.transpose(routes)
    named = jnp.zeros((ROWS, PARTNERS), F32)
    share = jnp.zeros((ROWS, PARTNERS), F32)
    for k in range(routes.shape[1]):
        match = routes[:, k : k + 1] == expert
        named = named + jnp.where(match, 1.0, 0.0)
        share = share + jnp.where(match, shares[:, k : k + 1], 0.0)
    below = (iota((ROWS, ROWS), 1) < iota((ROWS, ROWS), 0)).astype(F32).astype(BF16)
    code = named * (1.0 + dot(below, named.astype(BF16)))
    high = share.astype(BF16)
    low = (share - high.astype(F32)).astype(BF16)
    wide = PARTNERS * SLOT
    spread = jnp.where(iota((PARTNERS, wide), 1) // SLOT == iota((PARTNERS, wide), 0), 1.0, 0.0).astype(BF16)
    stacked = jnp.concatenate([code.astype(BF16), high, low], axis=0)
    lanes = dot(stacked, spread)
    lane = iota((ROWS, wide), 1)
    chosen = lanes[:ROWS] == ((lane & 1) + 1).astype(F32)
    parts = (
        jnp.where(chosen, 1.0, 0.0),
        jnp.where(chosen, lanes[ROWS : 2 * ROWS], 0.0),
        jnp.where(chosen, lanes[2 * ROWS :], 0.0),
    )
    block = (lane >> 1) & 7
    for c in range(8):
        here = block == c
        pick_ref[c * ROWS : (c + 1) * ROWS, :] = jnp.where(here, parts[0], 0.0).astype(BF16)
        mix_ref[c * ROWS : (c + 1) * ROWS, :] = jnp.where(here, parts[1], 0.0).astype(BF16)
        mix_ref[128 + c * ROWS : 128 + (c + 1) * ROWS, :] = jnp.where(here, parts[2], 0.0).astype(BF16)


def by_blocks(rows, halves):
    return jnp.concatenate(
        [
            jnp.concatenate(
                [rows[:, h * 1024 + c * 128 : h * 1024 + (c + 1) * 128] for h in range(halves)], axis=1
            )
            for c in range(8)
        ],
        axis=0,
    )


def unblock(blocks, halves):
    return jnp.concatenate(
        [
            blocks[c * ROWS : (c + 1) * ROWS, h * 128 : (h + 1) * 128]
            for h in range(halves)
            for c in range(8)
        ],
        axis=1,
    )


def copy_to(source, target, device, send_sem, recv_sem):
    return pltpu.make_async_remote_copy(
        src_ref=source,
        dst_ref=target,
        send_sem=send_sem,
        recv_sem=recv_sem,
        device_id=device,
        device_id_type=MESH,
    )


def wait_bytes(ref, first, last, sem):
    part = ref.at[pl.ds(first * SLOT, (last - first) * SLOT)]
    pltpu.make_async_copy(part, part, sem).wait()


def send_bins(place, order, bins, arrived, slots, chunks, send_sem, recv_sems):
    for j in slots:
        part = pl.ds(j * SLOT, SLOT)
        copy_to(
            bins.at[part], arrived.at[part], device_at(place, order[j], 1), send_sem, recv_sems.at[chunk_of(j, chunks)]
        ).start()


def chunk_of(j, chunks):
    return next(k for k, (first, last) in enumerate(chunks) if first <= j < last)


def fill_bins(g, pick, blocks, bins):
    lanes = pl.ds(g * 256, 256)
    bins[lanes, :] = lax.dot_general(
        pick[:, lanes], blocks, (((0,), (0,)), ((), ())), preferred_element_type=F32
    ).astype(BF16)


def run_expert(place, order, chunks, halves, mix, gate_up, down, bufs, sems):
    bins, arrived, rows, hidden, results, packed, returned = bufs
    there_recv, back_send, back_recv = sems
    width = halves * 1024
    own = pl.ds((PARTNERS - 1) * SLOT, SLOT)
    arrived[own, :] = bins[own, :]

    out_row, in_row = iota((256, 256), 0), iota((256, 256), 1)
    unpack = jnp.where(((out_row // 2) % 16) * 16 + (out_row // 32) * 2 + out_row % 2 == in_row, 1.0, 0.0).astype(BF16)
    pack = jnp.where(((in_row // 2) % 16) * 16 + (in_row // 32) * 2 + in_row % 2 == out_row, 1.0, 0.0).astype(BF16)
    hidden_width = down.shape[1]
    for k, (first, last) in enumerate(chunks):
        wait_bytes(arrived, first, min(last, PARTNERS - 1), there_recv.at[k])
        for g in range(first // 16, last // 16):
            group = dot(unpack, arrived[g * 256 : (g + 1) * 256, :]).astype(BF16)
            for h in range(halves):
                for c in range(8):
                    rows[g * 32 : (g + 1) * 32, h * 1024 + c * 128 : h * 1024 + (c + 1) * 128] = group[
                        c * 32 : (c + 1) * 32, h * 128 : (h + 1) * 128
                    ]
        span = slice(first * 2, last * 2)
        tile = 256 if hidden_width % 256 == 0 else 128
        for n in range(hidden_width // tile):
            gate = dot(rows[span, :], gate_up[0, :, n * tile : (n + 1) * tile])
            up = dot(rows[span, :], gate_up[0, :, hidden_width + n * tile : hidden_width + (n + 1) * tile])
            hidden[span, n * tile : (n + 1) * tile] = (gate / (1.0 + jnp.exp(-gate)) * up).astype(BF16)
        for n in range(width // 256):
            results[span, n * 256 : (n + 1) * 256] = dot(
                hidden[span, :], down[0, :, n * 256 : (n + 1) * 256]
            ).astype(BF16)
        for g in range(first // 16, last // 16):
            stacked = jnp.concatenate(
                [
                    jnp.concatenate(
                        [
                            results[g * 32 : (g + 1) * 32, h * 1024 + c * 128 : h * 1024 + (c + 1) * 128]
                            for h in range(halves)
                        ],
                        axis=1,
                    )
                    for c in range(8)
                ],
                axis=0,
            )
            packed[g * 256 : (g + 1) * 256, :] = dot(pack, stacked).astype(BF16)
            for j in range(g * 16, min(g * 16 + 16, PARTNERS - 1)):
                part = pl.ds(j * SLOT, SLOT)
                copy_to(packed.at[part], returned.at[part], device_at(place, order[j], -1), back_send, back_recv).start()
    returned[own, :] = packed[own, :]
    wait_bytes(returned, 0, PARTNERS - 1, back_recv)
    total = dot(mix[...], returned[...])
    return unblock(total[:128] + total[128:], halves)


def step_kernel(*refs):
    small, (gate_up1, down1, table_hbm, proj_hbm, gate_up2, down2) = refs[:11], refs[11:17]
    think_out, talk_out = refs[17:19]
    here, (gu1, dn1, table, proj, gu2, dn2) = refs[19:30], refs[30:36]
    think_row, talk_row, pick1, mix1, pick2, mix2 = refs[36:42]
    think_bufs, talk_bufs = refs[42:49], refs[49:56]
    small_sem, load_sem, send_sem, there_recv, back_recv, out_sem, relay_sem = refs[56:]
    steps, tokens, gain1, routes1, weights1, keep1, codec_ids, gain2, routes2, weights2, keep2 = here

    place = my_place()
    barrier = pltpu.get_barrier_semaphore()
    for step in NEAR:
        pl.semaphore_signal(barrier, inc=1, device_id=device_at(place, step, 1), device_id_type=MESH)
    smalls = [pltpu.make_async_copy(a, b, small_sem.at[i]) for i, (a, b) in enumerate(zip(small, here))]
    loads = [
        pltpu.make_async_copy(a, b, load_sem.at[i])
        for i, (a, b) in enumerate(
            zip((gate_up1, down1, table_hbm, proj_hbm, gate_up2, down2), (gu1, dn1, table, proj, gu2, dn2))
        )
    ]
    for load in smalls + loads:
        load.start()
    for load in smalls:
        load.wait()

    normed = rms_rows(tokens[...].astype(F32), gain1[...])
    route_tables(place, steps[0:1, :], routes1[...], weights1[...], keep1[...], pick1, mix1)
    bins, arrived = think_bufs[:2]
    blocks = by_blocks(normed, 2)
    for g in range(8):
        fill_bins(g, pick1, blocks, bins)
    pl.semaphore_wait(barrier, len(NEAR))
    for step in RELAYS:
        pl.semaphore_signal(relay_sem, inc=1, device_id=device_at(place, step, 1), device_id_type=MESH)
    send = functools.partial(send_bins, place, THINK_ORDER, bins, arrived)
    send(range(EARLY), THINK_CHUNKS, send_sem.at[0], there_recv.at[0])
    pl.semaphore_wait(relay_sem, len(RELAYS))
    send(range(EARLY, PARTNERS - 1), THINK_CHUNKS, send_sem.at[0], there_recv.at[0])

    route_tables(place, steps[1:2, :], routes2[...], weights2[...], keep2[...], pick2, mix2)
    loads[2].wait()
    vocab = table.shape[0]
    ids = jnp.transpose(jnp.broadcast_to(codec_ids[...], (8, ROWS)))[:, :1]
    chosen = jnp.where(iota((ROWS, vocab), 1) == ids, 1.0, 0.0).astype(BF16)
    codec = dot(chosen, table[...])
    loads[0].wait()
    loads[1].wait()
    mixed = run_expert(
        place,
        THINK_ORDER,
        THINK_CHUNKS,
        2,
        mix1,
        gu1,
        dn1,
        think_bufs,
        (there_recv.at[0], send_sem.at[1], back_recv.at[0]),
    )
    think = (tokens[...].astype(F32) + mixed).astype(BF16)
    think_row[...] = think
    think_store = pltpu.make_async_copy(think_row, think_out, out_sem.at[0])
    think_store.start()

    loads[3].wait()
    talk_input = dot(think, proj[...]) + codec
    blocks = by_blocks(rms_rows(talk_input, gain2[...]), 1)
    bins, arrived = talk_bufs[:2]
    for g in range(8):
        fill_bins(g, pick2, blocks, bins)
        slots = range(g * 16, min(g * 16 + 16, PARTNERS - 1))
        send_bins(place, TALK_ORDER, bins, arrived, slots, TALK_CHUNKS, send_sem.at[2], there_recv.at[1])
    loads[4].wait()
    loads[5].wait()
    mixed = run_expert(
        place,
        TALK_ORDER,
        TALK_CHUNKS,
        1,
        mix2,
        gu2,
        dn2,
        talk_bufs,
        (there_recv.at[1], send_sem.at[3], back_recv.at[1]),
    )
    talk_row[...] = (talk_input + mixed).astype(BF16)
    talk_store = pltpu.make_async_copy(talk_row, talk_out, out_sem.at[1])
    talk_store.start()
    for i, sent in enumerate((think_bufs[0], think_bufs[5], talk_bufs[0], talk_bufs[5])):
        wait_bytes(sent, 0, PARTNERS - 1, send_sem.at[i])
    think_store.wait()
    talk_store.wait()


def hand_over(think_in, talk_in, think_out, talk_out):
    think_out[...] = think_in[...]
    talk_out[...] = talk_in[...]


def shards(
    tokens,
    think_gain,
    think_routes,
    think_weights,
    think_keep,
    think_gate_up,
    think_down,
    talk_proj,
    codec_table,
    codec_ids,
    talk_gain,
    talk_routes,
    talk_weights,
    talk_keep,
    talk_gate_up,
    talk_down,
):
    steps = jnp.asarray(
        [[((a * 4 + c) * 4 + p) * 4 + q for a, c, p, q in order] for order in (THINK_ORDER, TALK_ORDER)], jnp.int32
    )
    wide = PARTNERS * SLOT
    hbm = pl.BlockSpec(memory_space=pltpu.HBM)
    small = (
        steps,
        tokens,
        think_gain.reshape(1, -1),
        think_routes.T,
        think_weights.T,
        think_keep.T,
        codec_ids.reshape(1, -1),
        talk_gain.reshape(1, -1),
        talk_routes.T,
        talk_weights.T,
        talk_keep.T,
    )
    large = (think_gate_up, think_down, codec_table, talk_proj, talk_gate_up, talk_down)
    outs = (
        jax.ShapeDtypeStruct(tokens.shape, BF16),
        jax.ShapeDtypeStruct((ROWS, talk_proj.shape[1]), BF16),
    )

    def exchange(halves, hidden_width):
        width = halves * 1024
        return [
            pltpu.VMEM((wide, halves * 128), BF16),
            pltpu.VMEM((wide, halves * 128), BF16),
            pltpu.VMEM((256, width), BF16),
            pltpu.VMEM((256, hidden_width), BF16),
            pltpu.VMEM((256, width), BF16),
            pltpu.VMEM((wide, halves * 128), BF16),
            pltpu.VMEM((wide, halves * 128), BF16),
        ]

    held = pl.pallas_call(
        step_kernel,
        out_shape=outs,
        in_specs=[hbm] * (len(small) + len(large)),
        out_specs=(hbm, hbm),
        scratch_shapes=[pltpu.VMEM(a.shape, a.dtype) for a in small + large + outs]
        + [pltpu.VMEM((rows, wide), BF16) for rows in (128, 256, 128, 256)]
        + exchange(2, think_down.shape[1])
        + exchange(1, talk_down.shape[1])
        + [
            pltpu.SemaphoreType.DMA((len(small),)),
            pltpu.SemaphoreType.DMA((len(large),)),
            pltpu.SemaphoreType.DMA((4,)),
            pltpu.SemaphoreType.DMA((2, max(len(THINK_CHUNKS), len(TALK_CHUNKS)))),
            pltpu.SemaphoreType.DMA((2,)),
            pltpu.SemaphoreType.DMA((2,)),
            pltpu.SemaphoreType.REGULAR,
        ],
        compiler_params=pltpu.CompilerParams(
            collective_id=0, has_side_effects=True, vmem_limit_bytes=56 * 2**20
        ),
        name="moe_step",
    )(*small, *large)
    return pl.pallas_call(hand_over, out_shape=outs, name="hand_over")(*held)


def solution(mesh):
    rows = P(AXES, None)
    experts = P(AXES, None, None)
    return jax.shard_map(
        shards,
        mesh=mesh,
        in_specs=(rows, P(), rows, rows, rows, experts, experts, P(), P(), P(AXES), P(), rows, rows, rows, experts, experts),
        out_specs=(rows, rows),
        check_vma=False,
    )
```

```python
import functools

import jax
import jax.numpy as jnp
import numpy as np
from jax import lax
from jax.experimental import pallas as pl
from jax.experimental.pallas import tpu as pltpu
from jax.sharding import PartitionSpec as P

MESH = pl.DeviceIdType.MESH
AXES = ("grp", "dp", "ep")
ROWS = 16
SLOT = 16
PARTNERS = 128
F32 = jnp.float32
BF16 = jnp.bfloat16


def hops(step):
    return sum(min(v, 4 - v) for v in step[1:])


def partner_order(distances):
    rng = np.random.default_rng(1)
    every = [(a, c, p, q) for a in range(2) for c in range(4) for p in range(4) for q in range(4)]
    shuffled = [every[i] for i in rng.permutation(len(every))]
    return sorted(shuffled, key=lambda step: distances.index(hops(step)) if any(step) else len(distances))


THINK_ORDER = partner_order((3, 6, 5, 4, 2, 1, 0))
TALK_ORDER = partner_order((6, 5, 4, 3, 2, 1, 0))
EARLY = sum(hops(step) == 3 for step in THINK_ORDER)
THINK_CHUNKS = ((0, 48), (48, 128))
TALK_CHUNKS = ((0, 48), (48, 128))
NEAR = [step for step in THINK_ORDER[:-1] if hops(step) <= 3]
RELAYS = ((0, 1, 1, 1), (0, 3, 3, 3))


def my_place():
    ep = lax.axis_index("ep")
    return lax.axis_index("grp"), lax.axis_index("dp"), ep // 4, ep % 4


def device_at(place, step, sign):
    grp, dp, x, y = place
    a, c, p, q = step
    if sign < 0:
        a, c, p, q = (-a) % 2, (-c) % 4, (-p) % 4, (-q) % 4
    return ((grp + a) % 2, (dp + c) % 4, ((x + p) % 4) * 4 + (y + q) % 4)


def iota(shape, dim):
    return lax.broadcasted_iota(jnp.int32, shape, dim)


def dot(a, b):
    return jnp.dot(a, b, preferred_element_type=F32)


def rms_rows(values, gain):
    inverse = lax.rsqrt(jnp.mean(values * values, axis=-1, keepdims=True) + 1e-06)
    return (values * inverse * gain).astype(BF16)


def route_tables(place, steps, routes, weights, keep, pick_ref, mix_ref):
    grp, dp, x, y = place
    expert = (
        (((grp + steps // 64) & 1) * 4 + ((dp + (steps // 16) % 4) & 3)) * 16
        + ((x + (steps // 4) % 4) & 3) * 4
        + ((y + steps % 4) & 3)
    )
    shares = jnp.transpose(weights * keep.astype(F32) / jnp.sum(weights, axis=0, keepdims=True))
    routes = jnp.transpose(routes)
    named = jnp.zeros((ROWS, PARTNERS), F32)
    share = jnp.zeros((ROWS, PARTNERS), F32)
    for k in range(routes.shape[1]):
        match = routes[:, k : k + 1] == expert
        named = named + jnp.where(match, 1.0, 0.0)
        share = share + jnp.where(match, shares[:, k : k + 1], 0.0)
    below = (iota((ROWS, ROWS), 1) < iota((ROWS, ROWS), 0)).astype(F32).astype(BF16)
    code = named * (1.0 + dot(below, named.astype(BF16)))
    high = share.astype(BF16)
    low = (share - high.astype(F32)).astype(BF16)
    wide = PARTNERS * SLOT
    spread = jnp.where(iota((PARTNERS, wide), 1) // SLOT == iota((PARTNERS, wide), 0), 1.0, 0.0).astype(BF16)
    stacked = jnp.concatenate([code.astype(BF16), high, low], axis=0)
    lanes = dot(stacked, spread)
    lane = iota((ROWS, wide), 1)
    chosen = lanes[:ROWS] == ((lane & 1) + 1).astype(F32)
    parts = (
        jnp.where(chosen, 1.0, 0.0),
        jnp.where(chosen, lanes[ROWS : 2 * ROWS], 0.0),
        jnp.where(chosen, lanes[2 * ROWS :], 0.0),
    )
    block = (lane >> 1) & 7
    for c in range(8):
        here = block == c
        pick_ref[c * ROWS : (c + 1) * ROWS, :] = jnp.where(here, parts[0], 0.0).astype(BF16)
        mix_ref[c * ROWS : (c + 1) * ROWS, :] = jnp.where(here, parts[1], 0.0).astype(BF16)
        mix_ref[128 + c * ROWS : 128 + (c + 1) * ROWS, :] = jnp.where(here, parts[2], 0.0).astype(BF16)


def by_blocks(rows, halves):
    return jnp.concatenate(
        [
            jnp.concatenate(
                [rows[:, h * 1024 + c * 128 : h * 1024 + (c + 1) * 128] for h in range(halves)], axis=1
            )
            for c in range(8)
        ],
        axis=0,
    )


def unblock(blocks, halves):
    return jnp.concatenate(
        [
            blocks[c * ROWS : (c + 1) * ROWS, h * 128 : (h + 1) * 128]
            for h in range(halves)
            for c in range(8)
        ],
        axis=1,
    )


def copy_to(source, target, device, send_sem, recv_sem):
    return pltpu.make_async_remote_copy(
        src_ref=source,
        dst_ref=target,
        send_sem=send_sem,
        recv_sem=recv_sem,
        device_id=device,
        device_id_type=MESH,
    )


def wait_bytes(ref, first, last, sem):
    part = ref.at[pl.ds(first * SLOT, (last - first) * SLOT)]
    pltpu.make_async_copy(part, part, sem).wait()


def send_bins(place, order, bins, arrived, slots, chunks, send_sem, recv_sems):
    for j in slots:
        part = pl.ds(j * SLOT, SLOT)
        copy_to(
            bins.at[part], arrived.at[part], device_at(place, order[j], 1), send_sem, recv_sems.at[chunk_of(j, chunks)]
        ).start()


def chunk_of(j, chunks):
    return next(k for k, (first, last) in enumerate(chunks) if first <= j < last)


def fill_bins(g, pick, blocks, bins):
    lanes = pl.ds(g * 256, 256)
    bins[lanes, :] = lax.dot_general(
        pick[:, lanes], blocks, (((0,), (0,)), ((), ())), preferred_element_type=F32
    ).astype(BF16)


def run_expert(place, order, chunks, halves, mix, gate_up, down, bufs, sems):
    bins, arrived, rows, hidden, results, packed, returned = bufs
    there_recv, back_send, back_recv = sems
    width = halves * 1024
    own = pl.ds((PARTNERS - 1) * SLOT, SLOT)
    arrived[own, :] = bins[own, :]

    out_row, in_row = iota((256, 256), 0), iota((256, 256), 1)
    unpack = jnp.where(((out_row // 2) % 16) * 16 + (out_row // 32) * 2 + out_row % 2 == in_row, 1.0, 0.0).astype(BF16)
    pack = jnp.where(((in_row // 2) % 16) * 16 + (in_row // 32) * 2 + in_row % 2 == out_row, 1.0, 0.0).astype(BF16)
    hidden_width = down.shape[1]
    for k, (first, last) in enumerate(chunks):
        wait_bytes(arrived, first, min(last, PARTNERS - 1), there_recv.at[k])
        for g in range(first // 16, last // 16):
            group = dot(unpack, arrived[g * 256 : (g + 1) * 256, :]).astype(BF16)
            for h in range(halves):
                for c in range(8):
                    rows[g * 32 : (g + 1) * 32, h * 1024 + c * 128 : h * 1024 + (c + 1) * 128] = group[
                        c * 32 : (c + 1) * 32, h * 128 : (h + 1) * 128
                    ]
        span = slice(first * 2, last * 2)
        tile = 256 if hidden_width % 256 == 0 else hidden_width
        for n in range(hidden_width // tile):
            if tile == hidden_width:
                both = dot(rows[span, :], gate_up[0])
                gate, up = both[:, :tile], both[:, tile:]
            else:
                gate = dot(rows[span, :], gate_up[0, :, n * tile : (n + 1) * tile])
                up = dot(rows[span, :], gate_up[0, :, hidden_width + n * tile : hidden_width + (n + 1) * tile])
            hidden[span, n * tile : (n + 1) * tile] = (gate / (1.0 + jnp.exp(-gate)) * up).astype(BF16)
        for n in range(width // 256):
            results[span, n * 256 : (n + 1) * 256] = dot(
                hidden[span, :], down[0, :, n * 256 : (n + 1) * 256]
            ).astype(BF16)
        for g in range(first // 16, last // 16):
            stacked = jnp.concatenate(
                [
                    jnp.concatenate(
                        [
                            results[g * 32 : (g + 1) * 32, h * 1024 + c * 128 : h * 1024 + (c + 1) * 128]
                            for h in range(halves)
                        ],
                        axis=1,
                    )
                    for c in range(8)
                ],
                axis=0,
            )
            packed[g * 256 : (g + 1) * 256, :] = dot(pack, stacked).astype(BF16)
            for j in range(g * 16, min(g * 16 + 16, PARTNERS - 1)):
                part = pl.ds(j * SLOT, SLOT)
                copy_to(packed.at[part], returned.at[part], device_at(place, order[j], -1), back_send, back_recv).start()
    returned[own, :] = packed[own, :]
    wait_bytes(returned, 0, PARTNERS - 1, back_recv)
    total = dot(mix[...], returned[...])
    return unblock(total[:128] + total[128:], halves)


def step_kernel(*refs):
    small, (gate_up1, down1, table_hbm, proj_hbm, gate_up2, down2) = refs[:11], refs[11:17]
    think_out, talk_out = refs[17:19]
    here, (gu1, dn1, table, proj, gu2, dn2) = refs[19:30], refs[30:36]
    think_row, talk_row, pick1, mix1, pick2, mix2 = refs[36:42]
    think_bufs, talk_bufs = refs[42:49], refs[49:56]
    small_sem, load_sem, send_sem, there_recv, back_recv, out_sem, relay_sem = refs[56:]
    steps, tokens, gain1, routes1, weights1, keep1, codec_ids, gain2, routes2, weights2, keep2 = here

    place = my_place()
    barrier = pltpu.get_barrier_semaphore()
    smalls = [pltpu.make_async_copy(a, b, small_sem.at[i]) for i, (a, b) in enumerate(zip(small, here))]
    loads = [
        pltpu.make_async_copy(a, b, load_sem.at[i])
        for i, (a, b) in enumerate(
            zip((gate_up1, down1, table_hbm, proj_hbm, gate_up2, down2), (gu1, dn1, table, proj, gu2, dn2))
        )
    ]
    for load in smalls:
        load.start()
    for step in NEAR:
        pl.semaphore_signal(barrier, inc=1, device_id=device_at(place, step, 1), device_id_type=MESH)
    for load in smalls:
        load.wait()

    normed = rms_rows(tokens[...].astype(F32), gain1[...])
    route_tables(place, steps[0:1, :], routes1[...], weights1[...], keep1[...], pick1, mix1)
    bins, arrived = think_bufs[:2]
    blocks = by_blocks(normed, 2)
    for g in range(8):
        fill_bins(g, pick1, blocks, bins)
    pl.semaphore_wait(barrier, len(NEAR))
    for step in RELAYS:
        pl.semaphore_signal(relay_sem, inc=1, device_id=device_at(place, step, 1), device_id_type=MESH)
    send = functools.partial(send_bins, place, THINK_ORDER, bins, arrived)
    send(range(EARLY), THINK_CHUNKS, send_sem.at[0], there_recv.at[0])
    pl.semaphore_wait(relay_sem, len(RELAYS))
    send(range(EARLY, PARTNERS - 1), THINK_CHUNKS, send_sem.at[0], there_recv.at[0])
    for load in loads:
        load.start()

    route_tables(place, steps[1:2, :], routes2[...], weights2[...], keep2[...], pick2, mix2)
    loads[2].wait()
    vocab = table.shape[0]
    ids = jnp.transpose(jnp.broadcast_to(codec_ids[...], (8, ROWS)))[:, :1]
    chosen = jnp.where(iota((ROWS, vocab), 1) == ids, 1.0, 0.0).astype(BF16)
    codec = dot(chosen, table[...])
    loads[0].wait()
    loads[1].wait()
    mixed = run_expert(
        place,
        THINK_ORDER,
        THINK_CHUNKS,
        2,
        mix1,
        gu1,
        dn1,
        think_bufs,
        (there_recv.at[0], send_sem.at[1], back_recv.at[0]),
    )
    think = (tokens[...].astype(F32) + mixed).astype(BF16)
    think_row[...] = think
    think_store = pltpu.make_async_copy(think_row, think_out, out_sem.at[0])
    think_store.start()

    loads[3].wait()
    talk_input = dot(think, proj[...]) + codec
    blocks = by_blocks(rms_rows(talk_input, gain2[...]), 1)
    bins, arrived = talk_bufs[:2]
    for g in range(8):
        fill_bins(g, pick2, blocks, bins)
        slots = range(g * 16, min(g * 16 + 16, PARTNERS - 1))
        send_bins(place, TALK_ORDER, bins, arrived, slots, TALK_CHUNKS, send_sem.at[2], there_recv.at[1])
    loads[4].wait()
    loads[5].wait()
    mixed = run_expert(
        place,
        TALK_ORDER,
        TALK_CHUNKS,
        1,
        mix2,
        gu2,
        dn2,
        talk_bufs,
        (there_recv.at[1], send_sem.at[3], back_recv.at[1]),
    )
    talk_row[...] = (talk_input + mixed).astype(BF16)
    talk_store = pltpu.make_async_copy(talk_row, talk_out, out_sem.at[1])
    talk_store.start()
    for i, sent in enumerate((think_bufs[0], think_bufs[5], talk_bufs[0], talk_bufs[5])):
        wait_bytes(sent, 0, PARTNERS - 1, send_sem.at[i])
    think_store.wait()
    talk_store.wait()


def hand_over(think_in, talk_in, think_out, talk_out):
    think_out[...] = think_in[...]
    talk_out[...] = talk_in[...]


def shards(
    tokens,
    think_gain,
    think_routes,
    think_weights,
    think_keep,
    think_gate_up,
    think_down,
    talk_proj,
    codec_table,
    codec_ids,
    talk_gain,
    talk_routes,
    talk_weights,
    talk_keep,
    talk_gate_up,
    talk_down,
):
    steps = jnp.asarray(
        [[((a * 4 + c) * 4 + p) * 4 + q for a, c, p, q in order] for order in (THINK_ORDER, TALK_ORDER)], jnp.int32
    )
    wide = PARTNERS * SLOT
    hbm = pl.BlockSpec(memory_space=pltpu.HBM)
    small = (
        steps,
        tokens,
        think_gain.reshape(1, -1),
        think_routes.T,
        think_weights.T,
        think_keep.T,
        codec_ids.reshape(1, -1),
        talk_gain.reshape(1, -1),
        talk_routes.T,
        talk_weights.T,
        talk_keep.T,
    )
    large = (think_gate_up, think_down, codec_table, talk_proj, talk_gate_up, talk_down)
    outs = (
        jax.ShapeDtypeStruct(tokens.shape, BF16),
        jax.ShapeDtypeStruct((ROWS, talk_proj.shape[1]), BF16),
    )

    def exchange(halves, hidden_width):
        width = halves * 1024
        return [
            pltpu.VMEM((wide, halves * 128), BF16),
            pltpu.VMEM((wide, halves * 128), BF16),
            pltpu.VMEM((256, width), BF16),
            pltpu.VMEM((256, hidden_width), BF16),
            pltpu.VMEM((256, width), BF16),
            pltpu.VMEM((wide, halves * 128), BF16),
            pltpu.VMEM((wide, halves * 128), BF16),
        ]

    held = pl.pallas_call(
        step_kernel,
        out_shape=outs,
        in_specs=[hbm] * (len(small) + len(large)),
        out_specs=(hbm, hbm),
        scratch_shapes=[pltpu.VMEM(a.shape, a.dtype) for a in small + large + outs]
        + [pltpu.VMEM((rows, wide), BF16) for rows in (128, 256, 128, 256)]
        + exchange(2, think_down.shape[1])
        + exchange(1, talk_down.shape[1])
        + [
            pltpu.SemaphoreType.DMA((len(small),)),
            pltpu.SemaphoreType.DMA((len(large),)),
            pltpu.SemaphoreType.DMA((4,)),
            pltpu.SemaphoreType.DMA((2, max(len(THINK_CHUNKS), len(TALK_CHUNKS)))),
            pltpu.SemaphoreType.DMA((2,)),
            pltpu.SemaphoreType.DMA((2,)),
            pltpu.SemaphoreType.REGULAR,
        ],
        compiler_params=pltpu.CompilerParams(
            collective_id=0, has_side_effects=True, vmem_limit_bytes=56 * 2**20
        ),
        name="moe_step",
    )(*small, *large)
    return pl.pallas_call(hand_over, out_shape=outs, name="hand_over")(*held)


def solution(mesh):
    rows = P(AXES, None)
    experts = P(AXES, None, None)
    return jax.shard_map(
        shards,
        mesh=mesh,
        in_specs=(rows, P(), rows, rows, rows, experts, experts, P(), P(), P(AXES), P(), rows, rows, rows, experts, experts),
        out_specs=(rows, rows),
        check_vma=False,
    )
```

```python
import functools

import jax
import jax.numpy as jnp
import numpy as np
from jax import lax
from jax.experimental import pallas as pl
from jax.experimental.pallas import tpu as pltpu
from jax.sharding import PartitionSpec as P

MESH = pl.DeviceIdType.MESH
AXES = ("grp", "dp", "ep")
ROWS = 16
SLOT = 16
PARTNERS = 128
F32 = jnp.float32
BF16 = jnp.bfloat16


def hops(step):
    return sum(min(v, 4 - v) for v in step[1:])


def partner_order(distances):
    rng = np.random.default_rng(1)
    every = [(a, c, p, q) for a in range(2) for c in range(4) for p in range(4) for q in range(4)]
    shuffled = [every[i] for i in rng.permutation(len(every))]
    return sorted(shuffled, key=lambda step: distances.index(hops(step)) if any(step) else len(distances))


THINK_ORDER = partner_order((3, 6, 5, 4, 2, 1, 0))
TALK_ORDER = partner_order((6, 5, 4, 3, 2, 1, 0))
EARLY = sum(hops(step) == 3 for step in THINK_ORDER)
THINK_CHUNKS = ((0, 48), (48, 128))
TALK_CHUNKS = ((0, 32), (32, 128))
NEAR = [step for step in THINK_ORDER[:-1] if hops(step) <= 3]
RELAYS = ((0, 1, 1, 1), (0, 3, 3, 3))


def my_place():
    ep = lax.axis_index("ep")
    return lax.axis_index("grp"), lax.axis_index("dp"), ep // 4, ep % 4


def device_at(place, step, sign):
    grp, dp, x, y = place
    a, c, p, q = step
    if sign < 0:
        a, c, p, q = (-a) % 2, (-c) % 4, (-p) % 4, (-q) % 4
    return ((grp + a) % 2, (dp + c) % 4, ((x + p) % 4) * 4 + (y + q) % 4)


def iota(shape, dim):
    return lax.broadcasted_iota(jnp.int32, shape, dim)


def dot(a, b):
    return jnp.dot(a, b, preferred_element_type=F32)


def rms_rows(values, gain):
    inverse = lax.rsqrt(jnp.mean(values * values, axis=-1, keepdims=True) + 1e-06)
    return (values * inverse * gain).astype(BF16)


def route_tables(place, steps, routes, weights, keep, pick_ref, mix_ref):
    grp, dp, x, y = place
    expert = (
        (((grp + steps // 64) & 1) * 4 + ((dp + (steps // 16) % 4) & 3)) * 16
        + ((x + (steps // 4) % 4) & 3) * 4
        + ((y + steps % 4) & 3)
    )
    shares = jnp.transpose(weights * keep.astype(F32) / jnp.sum(weights, axis=0, keepdims=True))
    routes = jnp.transpose(routes)
    named = jnp.zeros((ROWS, PARTNERS), F32)
    share = jnp.zeros((ROWS, PARTNERS), F32)
    for k in range(routes.shape[1]):
        match = routes[:, k : k + 1] == expert
        named = named + jnp.where(match, 1.0, 0.0)
        share = share + jnp.where(match, shares[:, k : k + 1], 0.0)
    below = (iota((ROWS, ROWS), 1) < iota((ROWS, ROWS), 0)).astype(F32).astype(BF16)
    code = named * (1.0 + dot(below, named.astype(BF16)))
    high = share.astype(BF16)
    low = (share - high.astype(F32)).astype(BF16)
    wide = PARTNERS * SLOT
    spread = jnp.where(iota((PARTNERS, wide), 1) // SLOT == iota((PARTNERS, wide), 0), 1.0, 0.0).astype(BF16)
    stacked = jnp.concatenate([code.astype(BF16), high, low], axis=0)
    lanes = dot(stacked, spread)
    lane = iota((ROWS, wide), 1)
    chosen = lanes[:ROWS] == ((lane & 1) + 1).astype(F32)
    parts = (
        jnp.where(chosen, 1.0, 0.0),
        jnp.where(chosen, lanes[ROWS : 2 * ROWS], 0.0),
        jnp.where(chosen, lanes[2 * ROWS :], 0.0),
    )
    block = (lane >> 1) & 7
    for c in range(8):
        here = block == c
        if pick_ref is not None:
            pick_ref[c * ROWS : (c + 1) * ROWS, :] = jnp.where(here, parts[0], 0.0).astype(BF16)
        if mix_ref is not None:
            mix_ref[c * ROWS : (c + 1) * ROWS, :] = jnp.where(here, parts[1], 0.0).astype(BF16)
            mix_ref[128 + c * ROWS : 128 + (c + 1) * ROWS, :] = jnp.where(here, parts[2], 0.0).astype(BF16)


def by_blocks(rows, halves):
    return jnp.concatenate(
        [
            jnp.concatenate(
                [rows[:, h * 1024 + c * 128 : h * 1024 + (c + 1) * 128] for h in range(halves)], axis=1
            )
            for c in range(8)
        ],
        axis=0,
    )


def unblock(blocks, halves):
    return jnp.concatenate(
        [
            blocks[c * ROWS : (c + 1) * ROWS, h * 128 : (h + 1) * 128]
            for h in range(halves)
            for c in range(8)
        ],
        axis=1,
    )


def copy_to(source, target, device, send_sem, recv_sem):
    return pltpu.make_async_remote_copy(
        src_ref=source,
        dst_ref=target,
        send_sem=send_sem,
        recv_sem=recv_sem,
        device_id=device,
        device_id_type=MESH,
    )


def wait_bytes(ref, first, last, sem):
    part = ref.at[pl.ds(first * SLOT, (last - first) * SLOT)]
    pltpu.make_async_copy(part, part, sem).wait()


def send_bins(place, order, bins, arrived, slots, chunks, send_sem, recv_sems):
    for j in slots:
        part = pl.ds(j * SLOT, SLOT)
        copy_to(
            bins.at[part], arrived.at[part], device_at(place, order[j], 1), send_sem, recv_sems.at[chunk_of(j, chunks)]
        ).start()


def chunk_of(j, chunks):
    return next(k for k, (first, last) in enumerate(chunks) if first <= j < last)


def fill_bins(g, pick, blocks, bins):
    lanes = pl.ds(g * 256, 256)
    bins[lanes, :] = lax.dot_general(
        pick[:, lanes], blocks, (((0,), (0,)), ((), ())), preferred_element_type=F32
    ).astype(BF16)


def run_expert(idle, place, order, chunks, halves, mix, gate_up, down, bufs, sems):
    bins, arrived, rows, hidden, results, packed, returned = bufs
    there_recv, back_send, back_recv = sems
    width = halves * 1024
    own = pl.ds((PARTNERS - 1) * SLOT, SLOT)
    arrived[own, :] = bins[own, :]

    out_row, in_row = iota((256, 256), 0), iota((256, 256), 1)
    unpack = jnp.where(((out_row // 2) % 16) * 16 + (out_row // 32) * 2 + out_row % 2 == in_row, 1.0, 0.0).astype(BF16)
    pack = jnp.where(((in_row // 2) % 16) * 16 + (in_row // 32) * 2 + in_row % 2 == out_row, 1.0, 0.0).astype(BF16)
    hidden_width = down.shape[1]
    for k, (first, last) in enumerate(chunks):
        wait_bytes(arrived, first, min(last, PARTNERS - 1), there_recv.at[k])
        for g in range(first // 16, last // 16):
            group = dot(unpack, arrived[g * 256 : (g + 1) * 256, :]).astype(BF16)
            for h in range(halves):
                for c in range(8):
                    rows[g * 32 : (g + 1) * 32, h * 1024 + c * 128 : h * 1024 + (c + 1) * 128] = group[
                        c * 32 : (c + 1) * 32, h * 128 : (h + 1) * 128
                    ]
        span = slice(first * 2, last * 2)
        tile = 256 if hidden_width % 256 == 0 else hidden_width
        for n in range(hidden_width // tile):
            if tile == hidden_width:
                both = dot(rows[span, :], gate_up[0])
                gate, up = both[:, :tile], both[:, tile:]
            else:
                gate = dot(rows[span, :], gate_up[0, :, n * tile : (n + 1) * tile])
                up = dot(rows[span, :], gate_up[0, :, hidden_width + n * tile : hidden_width + (n + 1) * tile])
            hidden[span, n * tile : (n + 1) * tile] = (gate / (1.0 + jnp.exp(-gate)) * up).astype(BF16)
        for n in range(width // 256):
            results[span, n * 256 : (n + 1) * 256] = dot(
                hidden[span, :], down[0, :, n * 256 : (n + 1) * 256]
            ).astype(BF16)
        for g in range(first // 16, last // 16):
            stacked = jnp.concatenate(
                [
                    jnp.concatenate(
                        [
                            results[g * 32 : (g + 1) * 32, h * 1024 + c * 128 : h * 1024 + (c + 1) * 128]
                            for h in range(halves)
                        ],
                        axis=1,
                    )
                    for c in range(8)
                ],
                axis=0,
            )
            packed[g * 256 : (g + 1) * 256, :] = dot(pack, stacked).astype(BF16)
            for j in range(g * 16, min(g * 16 + 16, PARTNERS - 1)):
                part = pl.ds(j * SLOT, SLOT)
                copy_to(packed.at[part], returned.at[part], device_at(place, order[j], -1), back_send, back_recv).start()
    returned[own, :] = packed[own, :]
    idle()
    wait_bytes(returned, 0, PARTNERS - 1, back_recv)
    total = dot(mix[...], returned[...])
    return unblock(total[:128] + total[128:], halves)


def step_kernel(*refs):
    small, (gate_up1, down1, table_hbm, proj_hbm, gate_up2, down2) = refs[:11], refs[11:17]
    think_out, talk_out = refs[17:19]
    here, (gu1, dn1, table, proj, gu2, dn2) = refs[19:30], refs[30:36]
    think_row, talk_row, pick1, mix1, pick2, mix2 = refs[36:42]
    think_bufs, talk_bufs = refs[42:49], refs[49:56]
    small_sem, load_sem, send_sem, there_recv, back_recv, out_sem, relay_sem, codec_row = refs[56:]
    steps, tokens, gain1, routes1, weights1, keep1, codec_ids, gain2, routes2, weights2, keep2 = here

    place = my_place()
    barrier = pltpu.get_barrier_semaphore()
    smalls = [pltpu.make_async_copy(a, b, small_sem.at[i]) for i, (a, b) in enumerate(zip(small, here))]
    loads = [
        pltpu.make_async_copy(a, b, load_sem.at[i])
        for i, (a, b) in enumerate(
            zip((gate_up1, down1, table_hbm, proj_hbm, gate_up2, down2), (gu1, dn1, table, proj, gu2, dn2))
        )
    ]
    for load in smalls:
        load.start()
    for step in NEAR:
        pl.semaphore_signal(barrier, inc=1, device_id=device_at(place, step, 1), device_id_type=MESH)
    for load in smalls:
        load.wait()
    for load in loads[:2]:
        load.start()

    normed = rms_rows(tokens[...].astype(F32), gain1[...])
    route_tables(place, steps[0:1, :], routes1[...], weights1[...], keep1[...], pick1, None)
    bins, arrived = think_bufs[:2]
    blocks = by_blocks(normed, 2)
    for g in range(8):
        fill_bins(g, pick1, blocks, bins)
    pl.semaphore_wait(barrier, len(NEAR))
    for step in RELAYS:
        pl.semaphore_signal(relay_sem, inc=1, device_id=device_at(place, step, 1), device_id_type=MESH)
    send = functools.partial(send_bins, place, THINK_ORDER, bins, arrived)
    send(range(EARLY), THINK_CHUNKS, send_sem.at[0], there_recv.at[0])
    pl.semaphore_wait(relay_sem, len(RELAYS))
    send(range(EARLY, PARTNERS - 1), THINK_CHUNKS, send_sem.at[0], there_recv.at[0])

    route_tables(place, steps[0:1, :], routes1[...], weights1[...], keep1[...], None, mix1)
    route_tables(place, steps[1:2, :], routes2[...], weights2[...], keep2[...], pick2, mix2)

    def find_codec():
        for load in loads[2:]:
            load.start()
        loads[2].wait()
        vocab = table.shape[0]
        ids = jnp.transpose(jnp.broadcast_to(codec_ids[...], (8, ROWS)))[:, :1]
        chosen = jnp.where(iota((ROWS, vocab), 1) == ids, 1.0, 0.0).astype(BF16)
        codec_row[...] = dot(chosen, table[...])

    loads[0].wait()
    loads[1].wait()
    mixed = run_expert(
        find_codec,
        place,
        THINK_ORDER,
        THINK_CHUNKS,
        2,
        mix1,
        gu1,
        dn1,
        think_bufs,
        (there_recv.at[0], send_sem.at[1], back_recv.at[0]),
    )
    think = (tokens[...].astype(F32) + mixed).astype(BF16)
    think_row[...] = think
    think_store = pltpu.make_async_copy(think_row, think_out, out_sem.at[0])
    think_store.start()

    loads[3].wait()
    talk_input = dot(think, proj[...]) + codec_row[...]
    blocks = by_blocks(rms_rows(talk_input, gain2[...]), 1)
    bins, arrived = talk_bufs[:2]
    for g in range(8):
        fill_bins(g, pick2, blocks, bins)
        slots = range(g * 16, min(g * 16 + 16, PARTNERS - 1))
        send_bins(place, TALK_ORDER, bins, arrived, slots, TALK_CHUNKS, send_sem.at[2], there_recv.at[1])
    loads[4].wait()
    loads[5].wait()
    mixed = run_expert(
        lambda: None,
        place,
        TALK_ORDER,
        TALK_CHUNKS,
        1,
        mix2,
        gu2,
        dn2,
        talk_bufs,
        (there_recv.at[1], send_sem.at[3], back_recv.at[1]),
    )
    talk_row[...] = (talk_input + mixed).astype(BF16)
    talk_store = pltpu.make_async_copy(talk_row, talk_out, out_sem.at[1])
    talk_store.start()
    for i, sent in enumerate((think_bufs[0], think_bufs[5], talk_bufs[0], talk_bufs[5])):
        wait_bytes(sent, 0, PARTNERS - 1, send_sem.at[i])
    think_store.wait()
    talk_store.wait()


def hand_over(think_in, talk_in, think_out, talk_out):
    think_out[...] = think_in[...]
    talk_out[...] = talk_in[...]


def shards(
    tokens,
    think_gain,
    think_routes,
    think_weights,
    think_keep,
    think_gate_up,
    think_down,
    talk_proj,
    codec_table,
    codec_ids,
    talk_gain,
    talk_routes,
    talk_weights,
    talk_keep,
    talk_gate_up,
    talk_down,
):
    steps = jnp.asarray(
        [[((a * 4 + c) * 4 + p) * 4 + q for a, c, p, q in order] for order in (THINK_ORDER, TALK_ORDER)], jnp.int32
    )
    wide = PARTNERS * SLOT
    hbm = pl.BlockSpec(memory_space=pltpu.HBM)
    small = (
        steps,
        tokens,
        think_gain.reshape(1, -1),
        think_routes.T,
        think_weights.T,
        think_keep.T,
        codec_ids.reshape(1, -1),
        talk_gain.reshape(1, -1),
        talk_routes.T,
        talk_weights.T,
        talk_keep.T,
    )
    large = (think_gate_up, think_down, codec_table, talk_proj, talk_gate_up, talk_down)
    outs = (
        jax.ShapeDtypeStruct(tokens.shape, BF16),
        jax.ShapeDtypeStruct((ROWS, talk_proj.shape[1]), BF16),
    )

    def exchange(halves, hidden_width):
        width = halves * 1024
        return [
            pltpu.VMEM((wide, halves * 128), BF16),
            pltpu.VMEM((wide, halves * 128), BF16),
            pltpu.VMEM((256, width), BF16),
            pltpu.VMEM((256, hidden_width), BF16),
            pltpu.VMEM((256, width), BF16),
            pltpu.VMEM((wide, halves * 128), BF16),
            pltpu.VMEM((wide, halves * 128), BF16),
        ]

    held = pl.pallas_call(
        step_kernel,
        out_shape=outs,
        in_specs=[hbm] * (len(small) + len(large)),
        out_specs=(hbm, hbm),
        scratch_shapes=[pltpu.VMEM(a.shape, a.dtype) for a in small + large + outs]
        + [pltpu.VMEM((rows, wide), BF16) for rows in (128, 256, 128, 256)]
        + exchange(2, think_down.shape[1])
        + exchange(1, talk_down.shape[1])
        + [
            pltpu.SemaphoreType.DMA((len(small),)),
            pltpu.SemaphoreType.DMA((len(large),)),
            pltpu.SemaphoreType.DMA((4,)),
            pltpu.SemaphoreType.DMA((2, max(len(THINK_CHUNKS), len(TALK_CHUNKS)))),
            pltpu.SemaphoreType.DMA((2,)),
            pltpu.SemaphoreType.DMA((2,)),
            pltpu.SemaphoreType.REGULAR,
            pltpu.VMEM((ROWS, talk_proj.shape[1]), F32),
        ],
        compiler_params=pltpu.CompilerParams(
            collective_id=0, has_side_effects=True, vmem_limit_bytes=56 * 2**20
        ),
        name="moe_step",
    )(*small, *large)
    return pl.pallas_call(hand_over, out_shape=outs, name="hand_over")(*held)


def solution(mesh):
    rows = P(AXES, None)
    experts = P(AXES, None, None)
    return jax.shard_map(
        shards,
        mesh=mesh,
        in_specs=(rows, P(), rows, rows, rows, experts, experts, P(), P(), P(AXES), P(), rows, rows, rows, experts, experts),
        out_specs=(rows, rows),
        check_vma=False,
    )
```
